32 devices in a mesh: band: 8 (over z, y), lev: 4 (over x, core).
Axes of the slice: x: 2, y: 2, z: 4, core: 2. Of those that a mesh axis runs over, the one named last changes fastest.
Arguments:
- spectral: float32 [672, 16, 128], P('band', 'lev'), may hold values from -6 to 6
- legendre: bfloat16 [672, 64, 128], P('band'), may hold values from -0.15625 to 0.15625
- wave_ids: int32 [64], P('band'), may hold values from 0 to 1279, as said below
- block_slot: int32 [672], P('band'), may hold values from 0 to 7, as said below
- block_start: int32 [672], P('band'), may hold values from 0 to 1216, as said below
- lat_weights: float32 [128], replicated, may hold values from 0.5 to 2
- drag: float32 [16, 2, 128], P('lev'), may hold values from 0.1 to 1
- mode_inverse: float32 [16, 16], replicated, may hold values from -1.5 to 1.5
- level_modes: float32 [16, 16], replicated, may hold values from -1.5 to 1.5
- depths: float32 [16], replicated, may hold values from 0.1 to 3
Outputs:
- spectral_next: float32 [672, 16, 128], P('band', 'lev')
The draws below stay inside these ranges and needn't reach their ends.
Inputs may be any that keep to these rules, and one draw needn't show every extreme that they name: `wave_ids`: distinct wavenumbers. The slots of index b of band, entries b * 8 to (b + 1) * 8 - 1, hold 4 pairs m and 1279 - m in some order; the pair 0 and 1279 is always present. `block_slot`: blocks b * 84 to (b + 1) * 84 - 1 belong to index b of band. For each slot of index b with wavenumber m there is exactly one block with each start 0, 64, 128, ... below 1280 - m, and no other block; the blocks stand in no particular order. `block_start`: A multiple of 64; see block_slot.
All inputs are finite; a program needn't handle non-finite values.
Results may differ from the reference program's by a relative error of at most 0.009.
Values may be sent and summed in bfloat16 or wider, within the bound.
A program may use at most 128 MiB of HBM per device.

```python
import math
import jax
import jax.numpy as jnp
from jax import lax

NTRUNC = 1280
NLON = 4096
LEV = 16
BLK = 64
WAVE_DEV = 8
WAVES = 64
BLK_DEV = 84
BLOCKS = 672
NLAT_H = 128


def pair_layout(key):
    base_key = jax.random.fold_in(key, 1729)
    device_count = WAVES // WAVE_DEV
    pair_count = WAVES // 2
    others = jax.random.permutation(jax.random.fold_in(base_key, 1), NTRUNC // 2 - 1).astype(jnp.int32) + 1
    low_waves = jnp.concatenate([jnp.zeros((1,), jnp.int32), others[:pair_count - 1]])
    low_waves = jax.random.permutation(jax.random.fold_in(base_key, 2), low_waves)
    high_waves = NTRUNC - 1 - low_waves
    owned = jnp.stack([low_waves, high_waves], axis=1).reshape(device_count, WAVE_DEV)
    device_keys = jax.random.split(jax.random.fold_in(base_key, 3), device_count)
    owned = jax.vmap(jax.random.permutation)(device_keys, owned)
    block_counts = (NTRUNC - owned + BLK - 1) // BLK
    block_ends = jnp.cumsum(block_counts, axis=1)
    begins = block_ends - block_counts
    positions = jnp.arange(BLK_DEV, dtype=jnp.int32)
    slot_of = jnp.sum((block_ends[:, None, :] <= positions[None, :, None]).astype(jnp.int32), axis=2)
    start_of = (positions[None, :] - jnp.take_along_axis(begins, slot_of, axis=1)) * BLK
    shuffle_keys = jax.random.split(jax.random.fold_in(base_key, 4), device_count)
    shuffle = jax.vmap(jax.random.permutation)(shuffle_keys, jnp.broadcast_to(positions, (device_count, BLK_DEV)))
    slot_of = jnp.take_along_axis(slot_of, shuffle, axis=1)
    start_of = jnp.take_along_axis(start_of, shuffle, axis=1)
    return (owned.reshape(WAVES).astype(jnp.int32), slot_of.reshape(device_count * BLK_DEV).astype(jnp.int32), start_of.reshape(device_count * BLK_DEV).astype(jnp.int32))


def draw_wave_ids(key, part):
    return pair_layout(key)[0]


def draw_block_slot(key, part):
    return pair_layout(key)[1]


def draw_block_start(key, part):
    return pair_layout(key)[2]


def levels(own_key, dims, cuts, least, top_value):
    loudness = 1.0
    for axis_at, shards_of in cuts:
        steps = jax.random.uniform(jax.random.fold_in(jax.random.fold_in(own_key, 6), axis_at), (shards_of,), jnp.float32, least / len(cuts), top_value / len(cuts))
        loudness = loudness * jnp.repeat(jnp.exp(steps), dims[axis_at] // shards_of).reshape((-1,) + (1,) * (len(dims) - 1 - axis_at))
    return loudness


def normal_values(stream_key, extent, width, bound, cuts=(), held_as=jnp.bfloat16):
    values = jax.random.normal(stream_key, extent, jnp.float32) * width
    if len(cuts) > 0:
        values = levels(stream_key, extent, cuts, -0.22, 0.18) * values
    return jnp.clip(values, min=-bound, max=bound).astype(held_as)


def setup_inputs(seed: int = 0) -> dict:
    key_list = jax.random.split(jax.random.key(seed), 11)
    spectral = normal_values(key_list[0], (BLOCKS, LEV, 2 * BLK), 1.0, 6.0, ((0, 8), (1, 4)), jnp.float32)
    legendre = normal_values(key_list[1], (BLOCKS, BLK, NLAT_H), NTRUNC ** -0.5, 0.15625, ((0, 8),))
    wave_ids = draw_wave_ids(jax.random.fold_in(key_list[10], 71), 0)
    block_slot = draw_block_slot(jax.random.fold_in(key_list[10], 71), 0)
    block_start = draw_block_start(jax.random.fold_in(key_list[10], 71), 0)
    lat_weights = jnp.clip(jnp.exp(jax.random.uniform(key_list[5], (NLAT_H,), jnp.float32, math.log(0.5), math.log(2.0))), 0.5, 2.0)
    drag = jnp.clip(jnp.exp(math.log(1.0) - 2.3025851 * jax.random.uniform(key_list[6], (LEV, 2, NLAT_H), jnp.float32) ** levels(key_list[6], (LEV, 2, NLAT_H), ((0, 4),), -0.2, 0.2)), 0.1, 1.0)
    mode_inverse = normal_values(key_list[7], (LEV, LEV), LEV ** -0.5, 1.5, (), jnp.float32)
    level_modes = normal_values(key_list[8], (LEV, LEV), LEV ** -0.5, 1.5, (), jnp.float32)
    depths = jnp.clip(jnp.exp(jax.random.uniform(key_list[9], (LEV,), jnp.float32, math.log(0.1), math.log(3.0))), 0.1, 3.0)
    return {"spectral": spectral, "legendre": legendre, "wave_ids": wave_ids, "block_slot": block_slot, "block_start": block_start, "lat_weights": lat_weights, "drag": drag, "mode_inverse": mode_inverse, "level_modes": level_modes, "depths": depths}


def row_offsets(row_count):
    half_rows = row_count // 2
    positions = jnp.arange(row_count, dtype=jnp.int32)
    return jnp.where(positions < half_rows, 2 * positions, 2 * (positions - half_rows) + 1)

def reference(spectral, legendre, wave_ids, block_slot, block_start, lat_weights, drag, mode_inverse, level_modes, depths):
    half_rows = BLK // 2
    groups = BLOCKS // BLK_DEV
    owner = jnp.arange(BLOCKS, dtype=jnp.int32) // BLK_DEV * WAVE_DEV + block_slot
    wave_of_block = jnp.take(wave_ids, owner)
    degree = wave_of_block[:, None] + block_start[:, None] + row_offsets(BLK)[None, :]
    live_rows = (degree < NTRUNC).astype(jnp.float32)
    live_cols = jnp.concatenate([live_rows, live_rows], axis=1)
    masked = spectral * live_cols[:, None, :]
    coeff = masked.astype(jnp.bfloat16)
    local_slots = jnp.arange(WAVE_DEV, dtype=jnp.int32)
    highest = lax.Precision.HIGHEST

    def inverse_group(pieces):
        group_coeff, group_legendre, group_slots = pieces
        split_coeff = group_coeff.astype(jnp.float32).reshape(BLK_DEV, LEV, 2, 2, half_rows)
        wide_legendre = group_legendre.astype(jnp.float32)
        even_part = jnp.einsum('klcr,kri->klci', split_coeff[:, :, :, 0, :], wide_legendre[:, :half_rows, :], precision=highest)
        odd_part = jnp.einsum('klcr,kri->klci', split_coeff[:, :, :, 1, :], wide_legendre[:, half_rows:, :], precision=highest)
        hemispheres = jnp.stack([even_part + odd_part, even_part - odd_part], axis=3)
        matches = (group_slots[:, None] == local_slots[None, :]).astype(jnp.float32)
        return jnp.einsum('ks,klchi->slchi', matches, hemispheres, precision=highest)
    fourier = lax.map(inverse_group, (coeff.reshape(groups, BLK_DEV, LEV, 2 * BLK), legendre.reshape(groups, BLK_DEV, BLK, NLAT_H), block_slot.reshape(groups, BLK_DEV)))
    fourier = fourier.reshape(WAVES, LEV, 2, 2, NLAT_H).astype(jnp.bfloat16)
    spectrum_len = NLON // 2 + 1
    real_scale = jnp.where(wave_ids == 0, NLON * 1.0, NLON * 0.5).astype(jnp.float32) / math.sqrt(WAVES)
    imag_scale = jnp.where(wave_ids == 0, 0.0, NLON * 0.5).astype(jnp.float32) / math.sqrt(WAVES)

    def grid_level(level_fourier):
        values = level_fourier.astype(jnp.float32)
        real_part = jnp.zeros((spectrum_len, 2, NLAT_H), jnp.float32).at[wave_ids].set(values[:, 0] * real_scale[:, None, None])
        imag_part = jnp.zeros((spectrum_len, 2, NLAT_H), jnp.float32).at[wave_ids].set(values[:, 1] * imag_scale[:, None, None])
        grid_values = jnp.fft.irfft(lax.complex(real_part, imag_part), n=NLON, axis=0)
        drag_force = grid_values * jnp.abs(grid_values)
        spectrum = jnp.fft.rfft(drag_force, axis=0)[wave_ids] / math.sqrt(NLON)
        return jnp.stack([jnp.real(spectrum), jnp.imag(spectrum)], axis=1).astype(jnp.bfloat16)
    drag_spec = lax.map(grid_level, jnp.moveaxis(fourier, 1, 0))
    drag_spec = jnp.moveaxis(drag_spec, 0, 1)
    northern = drag_spec[:, :, :, 0, :].astype(jnp.float32)
    southern = drag_spec[:, :, :, 1, :].astype(jnp.float32)
    drag_north = drag[:, 0, :][None, :, None, :]
    drag_south = drag[:, 1, :][None, :, None, :]
    weights_grid = lat_weights[None, None, None, :]
    symmetric = (-weights_grid * (drag_north * northern + drag_south * southern)).astype(jnp.bfloat16)
    antisymmetric = (-weights_grid * (drag_north * northern - drag_south * southern)).astype(jnp.bfloat16)
    degree_f = degree.astype(jnp.float32)
    growth = degree_f * (degree_f + 1.0) / (NTRUNC * NTRUNC)
    growth = jnp.concatenate([growth, growth], axis=1)

    def direct_group(pieces):
        group_legendre, group_slots, group_sym, group_anti, group_masked, group_live, group_growth = pieces
        wide_legendre = group_legendre.astype(jnp.float32)
        sym_blocks = jnp.take(group_sym, group_slots, axis=0).astype(jnp.float32)
        anti_blocks = jnp.take(group_anti, group_slots, axis=0).astype(jnp.float32)
        even_part = jnp.einsum('klci,kri->klcr', sym_blocks, wide_legendre[:, :half_rows, :], precision=highest)
        odd_part = jnp.einsum('klci,kri->klcr', anti_blocks, wide_legendre[:, half_rows:, :], precision=highest)
        tendency = jnp.stack([even_part, odd_part], axis=3).reshape(BLK_DEV, LEV, 2 * BLK) * group_live[:, None, :]
        combined = group_masked + tendency
        modal = jnp.einsum('al,klx->kax', mode_inverse, combined, precision=highest)
        implicit_gain = 1.0 / (1.0 + depths[None, :, None] * group_growth[:, None, :])
        return jnp.einsum('la,kax->klx', level_modes, modal * implicit_gain, precision=highest)
    result = lax.map(direct_group, (legendre.reshape(groups, BLK_DEV, BLK, NLAT_H), block_slot.reshape(groups, BLK_DEV), symmetric.reshape(groups, WAVE_DEV, LEV, 2, NLAT_H), antisymmetric.reshape(groups, WAVE_DEV, LEV, 2, NLAT_H), masked.reshape(groups, BLK_DEV, LEV, 2 * BLK), live_cols.reshape(groups, BLK_DEV, 2 * BLK), growth.reshape(groups, BLK_DEV, 2 * BLK)))
    return result.reshape(BLOCKS, LEV, 2 * BLK)
```

```python
import functools
import math

import jax
import jax.numpy as jnp
from jax import lax
from jax.experimental import pallas as pl
from jax.experimental.pallas import tpu as pltpu
from jax.sharding import PartitionSpec as P

NTRUNC = 1280
NLON = 4096
LANES = 128
MESH = pl.DeviceIdType.MESH
NT = (((1,), (1,)), ((), ()))
F32 = jnp.float32
BF16 = jnp.bfloat16


def iota(shape, dim):
    return lax.broadcasted_iota(jnp.int32, shape, dim)


def whole_div(values, divisor):
    return jnp.floor((values.astype(F32) + 0.5) * (1.0 / divisor)).astype(jnp.int32)


def whole_mod(values, divisor):
    return values - divisor * whole_div(values, divisor)


def kernel(
    band_size,
    lev_size,
    chunk_blocks,
    waves_ref,
    slot_ref,
    start_ref,
    depth_ref,
    x_ref,
    leg_ref,
    weight_ref,
    drag_ref,
    inverse_ref,
    modes_ref,
    out_ref,
    wave_all,
    outgoing,
    incoming,
    leaving,
    returned,
    twiddle,
    picked,
    picks,
    degree,
    mixed,
    gathered,
    gain,
    wave_sems,
    go_sems,
    back_sems,
    lev_sems,
):
    band = lax.axis_index("band")
    lev = lax.axis_index("lev")
    block_count, row_count, lat_pairs = leg_ref.shape
    half = row_count // 2
    levels = x_ref.shape[0] // block_count
    all_levels = levels * lev_size
    slots = waves_ref.shape[0]
    pair = 2 * slots
    lat_chunks = lat_pairs // LANES
    wave_rows = band_size * pair
    chunks = block_count // chunk_blocks
    chunk_rows = chunk_blocks * levels

    barrier = pltpu.get_barrier_semaphore()
    for step in range(1, band_size):
        pl.semaphore_signal(
            barrier, inc=1, device_id={"band": lax.rem(band + step, band_size)}, device_id_type=MESH
        )
    for step in range(1, lev_size):
        pl.semaphore_signal(
            barrier, inc=1, device_id={"lev": lax.rem(lev + step, lev_size)}, device_id_type=MESH
        )

    row16 = iota((pair, LANES), 0)
    own_waves = jnp.zeros((pair, LANES), jnp.int32)
    for s in range(slots):
        own_waves = jnp.where((row16 == s) | (row16 == s + slots), waves_ref[s], own_waves)
    wave_all[band] = own_waves
    pl.semaphore_wait(barrier, band_size + lev_size - 2)

    def band_copies(source, target, sems, by_peer):
        copies = []
        for step in range(1, band_size):
            peer = lax.rem(band + step, band_size)
            copies.append(
                pltpu.make_async_remote_copy(
                    src_ref=source.at[peer] if by_peer else source.at[band],
                    dst_ref=target.at[band],
                    send_sem=sems.at[0, step],
                    recv_sem=sems.at[1, step],
                    device_id={"band": peer},
                    device_id_type=MESH,
                )
            )
        for copy in copies:
            copy.start()
        return copies

    wave_copies = band_copies(wave_all, wave_all, wave_sems, False)

    lane = iota((1, LANES), 1)
    in_row = jnp.where(lane < row_count, lane, lane - row_count)
    even_lane = in_row < half
    real_lane = lane < row_count
    offset = jnp.where(even_lane, 2 * in_row, 2 * (in_row - half) + 1)

    slot_row = iota((slots, LANES), 0)
    lane8 = iota((slots, LANES), 1)
    in8 = jnp.where(lane8 < row_count, lane8, lane8 - row_count)
    parts = [
        (lane8 < row_count) & (in8 < half),
        (lane8 >= row_count) & (in8 < half),
        (lane8 < row_count) & (in8 >= half),
        (lane8 >= row_count) & (in8 >= half),
    ]

    slot_degree = own_waves[:slots] + offset

    def forward_lhs(k, first):
        own = slot_row == slot_ref[k]
        reached = slot_degree + start_ref[k]
        if first:
            degree[pl.ds(k, 1), :] = jnp.sum(
                jnp.where(own, reached, 0).astype(F32), axis=0, keepdims=True
            )
        own = own & (reached < NTRUNC)
        pieces = []
        rows = [jnp.where(own, x_ref[pl.ds(k * levels + l, 1), :], 0.0) for l in range(levels)]
        for parity in range(2):
            for l in range(levels):
                for c in range(2):
                    pieces.append(jnp.where(parts[2 * parity + c], rows[l], 0.0))
        return jnp.concatenate(pieces, axis=0).astype(BF16)

    group = 4
    for ic in range(lat_chunks):
        cols = pl.ds(ic * LANES, LANES)

        def forward(g, total, cols=cols, first_pass=ic == 0):
            for u in range(0, group, 2):
                k = g * group + u
                lhs = jnp.concatenate(
                    [forward_lhs(k, first_pass), forward_lhs(k + 1, first_pass)], axis=1
                )
                first, second = leg_ref[k, :, cols], leg_ref[k + 1, :, cols]
                rhs = jnp.concatenate([first, first, second, second], axis=0)
                total = total + jnp.dot(lhs, rhs, preferred_element_type=F32)
            return total

        total = lax.fori_loop(
            0, block_count // group, forward, jnp.zeros((2 * levels * pair, LANES), F32)
        )
        for l in range(levels):
            even = total[l * pair : (l + 1) * pair]
            odd = total[(levels + l) * pair : (levels + l + 1) * pair]
            outgoing[(2 * l) * lat_chunks + ic] = (even + odd).astype(BF16)
            outgoing[(2 * l + 1) * lat_chunks + ic] = (even - odd).astype(BF16)
    go_copies = band_copies(outgoing, incoming, go_sems, True)
    incoming[band] = outgoing[band]

    for copy in wave_copies:
        copy.wait()
    turn = 2.0 * math.pi / NLON
    row_block = min(wave_rows, 128)
    peers_in = row_block // pair

    def twiddle_rows(t):
        wave = jnp.concatenate([wave_all[t * peers_in + p] for p in range(peers_in)], axis=0)
        lanes = iota((row_block, LANES), 1)
        real = (iota((row_block, LANES), 0) & (pair - 1)) < slots
        coarse = ((wave * lanes * LANES) & (NLON - 1)).astype(F32) * turn
        fine = ((wave * lanes) & (NLON - 1)).astype(F32) * turn
        cos_c, sin_c = jnp.cos(coarse), jnp.sin(coarse)
        lead, trail = jnp.where(real, cos_c, -sin_c), jnp.where(real, sin_c, cos_c)
        cos_f, sin_f = jnp.cos(fine), jnp.sin(fine)
        rows = pl.ds(t * row_block, row_block)
        for a in range(NLON // LANES):
            values = lead[:, a : a + 1] * cos_f - trail[:, a : a + 1] * sin_f
            twiddle[rows, pl.ds(a * LANES, LANES)] = values.astype(BF16)

    for t in range(wave_rows // row_block):
        twiddle_rows(t)
    for copy in go_copies:
        copy.wait()

    field = jnp.concatenate([incoming[p] for p in range(band_size)], axis=0)
    field = field.astype(F32).T.astype(BF16)
    width = 512

    def drag_block(j, total):
        cols = pl.ds(pl.multiple_of(j * width, width), width)
        table = twiddle[:, cols]
        values = jnp.dot(field, table, preferred_element_type=F32)
        force = (values * jnp.abs(values)).astype(BF16)
        return total + lax.dot_general(table, force, NT, preferred_element_type=F32)

    spectrum = lax.fori_loop(
        0, NLON // width, drag_block, jnp.zeros((wave_rows, LANES), F32), unroll=True
    )
    spectrum = (spectrum * (1.0 / (band_size * slots * math.sqrt(NLON)))).astype(BF16)
    for p in range(band_size):
        leaving[p] = spectrum[p * pair : (p + 1) * pair]
    back_copies = band_copies(leaving, returned, back_sems, True)
    returned[band] = leaving[band]

    modal_rows = chunk_blocks * all_levels
    r_of, c_of = iota((modal_rows, all_levels), 0), iota((modal_rows, all_levels), 1)
    spread = (whole_mod(r_of, all_levels) == c_of).astype(F32).astype(BF16)
    l_of, q_of = iota((all_levels, modal_rows), 0), iota((all_levels, modal_rows), 1)
    level_of = levels * whole_div(q_of, chunk_rows) + whole_mod(q_of, levels)
    collect = (l_of == level_of).astype(F32).astype(BF16)
    left = jnp.dot(spread, inverse_ref[...].astype(BF16), preferred_element_type=F32).astype(BF16)
    left = jnp.dot(left, collect, preferred_element_type=F32)
    r_of, c_of = iota((modal_rows, modal_rows), 0), iota((modal_rows, modal_rows), 1)
    same = whole_div(r_of, all_levels) == whole_div(whole_mod(c_of, chunk_rows), levels)
    to_modes = jnp.where(same, left, 0.0).astype(BF16)
    r_of, c_of = iota((chunk_rows, all_levels), 0), iota((chunk_rows, all_levels), 1)
    spread = (c_of == lev * levels + whole_mod(r_of, levels)).astype(F32).astype(BF16)
    collect = (l_of == whole_mod(q_of, all_levels)).astype(F32).astype(BF16)
    right = jnp.dot(spread, modes_ref[...].astype(BF16), preferred_element_type=F32).astype(BF16)
    right = jnp.dot(right, collect, preferred_element_type=F32)
    r_of, c_of = iota((chunk_rows, modal_rows), 0), iota((chunk_rows, modal_rows), 1)
    same = whole_div(r_of, levels) == whole_div(c_of, all_levels)
    from_modes = jnp.where(same, right, 0.0).astype(BF16)

    mode_row = iota((all_levels, LANES), 0)
    depth = jnp.zeros((all_levels, LANES), F32)
    for a in range(all_levels):
        depth = jnp.where(mode_row == a, depth_ref[a], depth)

    kinds = 4 * levels
    kind_lane = iota((kinds, kinds * slots), 1)
    lane_slot = whole_mod(kind_lane, slots)
    kind = whole_div(kind_lane, slots) == iota((kinds, kinds * slots), 0)

    def gain_block(g, carry):
        for u in range(group):
            k = g * group + u
            n = degree[pl.ds(k, 1), :]
            growth = n * (n + 1.0) * (1.0 / (NTRUNC * NTRUNC))
            rows = pl.ds(pl.multiple_of(k * all_levels, all_levels), all_levels)
            gain[rows, :] = 1.0 / (1.0 + depth * growth)
            rows = pl.ds(pl.multiple_of(k * 4 * levels, 16), 4 * levels)
            picks[rows, :] = jnp.where(kind & (lane_slot == slot_ref[k]), 1.0, 0.0).astype(BF16)
        return carry

    lax.fori_loop(0, block_count // group, gain_block, 0)
    for copy in back_copies:
        copy.wait()

    for ic in range(lat_chunks):
        columns = [None] * kinds
        weight = -weight_ref[:, ic * LANES : (ic + 1) * LANES]
        for l in range(levels):
            north = returned[(2 * l) * lat_chunks + ic].astype(F32)
            south = returned[(2 * l + 1) * lat_chunks + ic].astype(F32)
            drag_n = drag_ref[2 * l : 2 * l + 1, ic * LANES : (ic + 1) * LANES]
            drag_s = drag_ref[2 * l + 1 : 2 * l + 2, ic * LANES : (ic + 1) * LANES]
            north, south = drag_n * north, drag_s * south
            for parity, value in enumerate((weight * (north + south), weight * (north - south))):
                for c in range(2):
                    at = (parity * 2 + c) * levels + l
                    columns[at] = value[c * slots : (c + 1) * slots]

        picked[ic] = jnp.concatenate(columns, axis=0).astype(BF16)

    def lev_copies(j):
        rows = pl.ds(pl.multiple_of(j * chunk_rows, chunk_rows), chunk_rows)
        return [
            pltpu.make_async_remote_copy(
                src_ref=gathered.at[lev, rows],
                dst_ref=gathered.at[lev, rows],
                send_sem=lev_sems.at[0, step, j],
                recv_sem=lev_sems.at[1, step, j],
                device_id={"lev": lax.rem(lev + step, lev_size)},
                device_id_type=MESH,
            )
            for step in range(1, lev_size)
        ]

    def direct_chunk(j, carry):
        pick_rows = pl.ds(pl.multiple_of(j * chunk_blocks * kinds, 16), chunk_blocks * kinds)
        chosen_rows = [
            jnp.dot(picks[pick_rows, :], picked[ic], preferred_element_type=F32).astype(BF16)
            for ic in range(lat_chunks)
        ]
        for u in range(0, chunk_blocks, 2):
            k = j * chunk_blocks + u
            product = None
            for ic in range(lat_chunks):
                cols = pl.ds(ic * LANES, LANES)
                lhs = chosen_rows[ic][u * kinds : (u + 2) * kinds]
                first, second = leg_ref[k, :, cols], leg_ref[k + 1, :, cols]
                rhs = jnp.concatenate([first, first, second, second], axis=0)
                term = lax.dot_general(lhs, rhs, NT, preferred_element_type=F32)
                product = term if product is None else product + term
            for v in range(2):
                own = product[v * 4 * levels : (v + 1) * 4 * levels, v * LANES : (v + 1) * LANES]
                chosen = jnp.where(even_lane, own[: 2 * levels], own[2 * levels :])
                tendency = jnp.where(real_lane, chosen[:levels], chosen[levels:])
                live = degree[pl.ds(k + v, 1), :] < NTRUNC
                rows = pl.ds((k + v) * levels, levels)
                mixed[rows, :] = jnp.where(live, x_ref[rows, :] + tendency, 0.0)
        rows = pl.ds(pl.multiple_of(j * chunk_rows, chunk_rows), chunk_rows)
        gathered[lev, rows, :] = mixed[rows, :].astype(BF16)
        for copy in lev_copies(j):
            copy.start()
        return carry

    lax.fori_loop(0, chunks, direct_chunk, 0)

    def solve_chunk(j, carry):
        for copy in lev_copies(j):
            copy.wait()
        rows = pl.ds(pl.multiple_of(j * chunk_rows, chunk_rows), chunk_rows)
        columns = jnp.concatenate([gathered[q, rows, :] for q in range(lev_size)], axis=0)
        modal = jnp.dot(to_modes, columns, preferred_element_type=F32)
        gains = gain[pl.ds(pl.multiple_of(j * modal_rows, modal_rows), modal_rows), :]
        out_ref[rows, :] = jnp.dot(
            from_modes, (modal * gains).astype(BF16), preferred_element_type=F32
        )
        return carry

    lax.fori_loop(0, chunks, solve_chunk, 0)


def on_device(band_size, lev_size, *args):
    spectral, legendre, waves, slot, start, weights, drag, inverse, modes, depths = args
    block_count, levels, columns = spectral.shape
    lat_pairs = legendre.shape[2]
    slots, all_levels = waves.shape[0], inverse.shape[0]
    pair = 2 * slots
    rows = block_count * levels
    chunk_blocks = max(
        n
        for n in range(2, 17, 2)
        if block_count % n == 0 and n * levels % 16 == 0
    )
    chunks = block_count // chunk_blocks
    assert levels * 2 * lat_pairs == band_size * LANES and columns == LANES
    smem = pl.BlockSpec(memory_space=pltpu.SMEM)
    vmem = pl.BlockSpec(memory_space=pltpu.VMEM)
    box = (band_size, pair, LANES)
    result = pl.pallas_call(
        functools.partial(kernel, band_size, lev_size, chunk_blocks),
        out_shape=jax.ShapeDtypeStruct((rows, LANES), F32),
        in_specs=[smem] * 4 + [vmem] * 6,
        out_specs=vmem,
        scratch_shapes=[
            pltpu.VMEM(box, jnp.int32),
            pltpu.VMEM(box, BF16),
            pltpu.VMEM(box, BF16),
            pltpu.VMEM(box, BF16),
            pltpu.VMEM(box, BF16),
            pltpu.VMEM((band_size * pair, NLON), BF16),
            pltpu.VMEM((lat_pairs // LANES, slots * 4 * levels, LANES), BF16),
            pltpu.VMEM((rows * 4, slots * 4 * levels), BF16),
            pltpu.VMEM((block_count, LANES), F32),
            pltpu.VMEM((rows, LANES), F32),
            pltpu.VMEM((lev_size, rows, LANES), BF16),
            pltpu.VMEM((block_count * all_levels, LANES), F32),
            pltpu.SemaphoreType.DMA((2, band_size)),
            pltpu.SemaphoreType.DMA((2, band_size)),
            pltpu.SemaphoreType.DMA((2, band_size)),
            pltpu.SemaphoreType.DMA((2, lev_size, chunks)),
        ],
        compiler_params=pltpu.CompilerParams(
            collective_id=0, has_side_effects=True, vmem_limit_bytes=48 * 2**20
        ),
    )(
        waves,
        slot,
        start,
        depths,
        spectral.reshape(rows, LANES),
        legendre,
        weights.reshape(1, lat_pairs),
        drag.reshape(levels * 2, lat_pairs),
        inverse,
        modes,
    )
    return result.reshape(spectral.shape)


def solution(mesh):
    placed = (
        P("band", "lev", None),
        P("band", None, None),
        P("band"),
        P("band"),
        P("band"),
        P(),
        P("lev", None, None),
        P(),
        P(),
        P(),
    )
    return jax.shard_map(
        functools.partial(on_device, mesh.shape["band"], mesh.shape["lev"]),
        mesh=mesh,
        in_specs=placed,
        out_specs=P("band", "lev", None),
        check_vma=False,
    )
```

```python
import functools
import math

import jax
import jax.numpy as jnp
from jax import lax
from jax.experimental import pallas as pl
from jax.experimental.pallas import tpu as pltpu
from jax.sharding import PartitionSpec as P

NTRUNC = 1280
NLON = 4096
LANES = 128
MESH = pl.DeviceIdType.MESH
NT = (((1,), (1,)), ((), ()))
F32 = jnp.float32
BF16 = jnp.bfloat16


def iota(shape, dim):
    return lax.broadcasted_iota(jnp.int32, shape, dim)


def whole_div(values, divisor):
    return jnp.floor((values.astype(F32) + 0.5) * (1.0 / divisor)).astype(jnp.int32)


def whole_mod(values, divisor):
    return values - divisor * whole_div(values, divisor)


def turns(phase):
    phase = ((phase + NLON // 2) & (NLON - 1)) - NLON // 2
    y = phase.astype(F32) * (math.pi / NLON)
    z = y * y
    sine, cosine = jnp.zeros_like(z), jnp.zeros_like(z)
    for n in reversed(range(7)):
        sine = sine * z + (-1) ** n / math.factorial(2 * n + 1)
        cosine = cosine * z + (-1) ** n / math.factorial(2 * n)
    sine = sine * y
    return 1.0 - 2.0 * sine * sine, 2.0 * sine * cosine


def kernel(
    band_size,
    lev_size,
    chunk_blocks,
    waves_hbm,
    slot_hbm,
    start_hbm,
    depth_hbm,
    x_hbm,
    leg_hbm,
    weight_hbm,
    drag_hbm,
    inverse_hbm,
    modes_hbm,
    out_ref,
    wave_all,
    outgoing,
    incoming,
    leaving,
    returned,
    twiddle,
    picked,
    picks,
    degree,
    mixed,
    gathered,
    gain,
    waves_ref,
    slot_ref,
    start_ref,
    depth_ref,
    x_ref,
    leg_ref,
    weight_ref,
    drag_ref,
    inverse_ref,
    modes_ref,
    load_sems,
    wave_sems,
    go_sems,
    back_sems,
    lev_sems,
):
    band = lax.axis_index("band")
    lev = lax.axis_index("lev")
    block_count, row_count, lat_pairs = leg_ref.shape
    half = row_count // 2
    levels = x_ref.shape[0] // block_count
    all_levels = levels * lev_size
    slots = waves_ref.shape[0]
    pair = 2 * slots
    lat_chunks = lat_pairs // LANES
    wave_rows = band_size * pair
    chunks = block_count // chunk_blocks
    chunk_rows = chunk_blocks * levels

    loads = [
        pltpu.make_async_copy(source, target, load_sems.at[n])
        for n, (source, target) in enumerate(
            (
                (waves_hbm, waves_ref),
                (slot_hbm, slot_ref),
                (start_hbm, start_ref),
                (x_hbm, x_ref),
                (leg_hbm, leg_ref),
                (depth_hbm, depth_ref),
                (weight_hbm, weight_ref),
                (drag_hbm, drag_ref),
                (inverse_hbm, inverse_ref),
                (modes_hbm, modes_ref),
            )
        )
    ]
    barrier = pltpu.get_barrier_semaphore()
    for step in range(1, band_size):
        pl.semaphore_signal(
            barrier, inc=1, device_id={"band": lax.rem(band + step, band_size)}, device_id_type=MESH
        )
    for step in range(1, lev_size):
        pl.semaphore_signal(
            barrier, inc=1, device_id={"lev": lax.rem(lev + step, lev_size)}, device_id_type=MESH
        )

    for load in loads:
        load.start()
    loads[0].wait()
    row16 = iota((pair, LANES), 0)
    own_waves = jnp.zeros((pair, LANES), jnp.int32)
    for s in range(slots):
        own_waves = jnp.where((row16 == s) | (row16 == s + slots), waves_ref[s], own_waves)
    wave_all[band] = own_waves
    pl.semaphore_wait(barrier, band_size + lev_size - 2)

    def band_copies(source, target, sems, by_peer):
        copies = []
        for step in range(1, band_size):
            peer = lax.rem(band + step, band_size)
            copies.append(
                pltpu.make_async_remote_copy(
                    src_ref=source.at[peer] if by_peer else source.at[band],
                    dst_ref=target.at[band],
                    send_sem=sems.at[0, step],
                    recv_sem=sems.at[1, step],
                    device_id={"band": peer},
                    device_id_type=MESH,
                )
            )
        for copy in copies:
            copy.start()
        return copies

    wave_copies = band_copies(wave_all, wave_all, wave_sems, False)
    for load in loads[1:]:
        load.wait()

    lane = iota((1, LANES), 1)
    in_row = jnp.where(lane < row_count, lane, lane - row_count)
    even_lane = in_row < half
    real_lane = lane < row_count
    offset = jnp.where(even_lane, 2 * in_row, 2 * (in_row - half) + 1)

    slot_row = iota((slots, LANES), 0)
    lane8 = iota((slots, LANES), 1)
    in8 = jnp.where(lane8 < row_count, lane8, lane8 - row_count)
    parts = [
        (lane8 < row_count) & (in8 < half),
        (lane8 >= row_count) & (in8 < half),
        (lane8 < row_count) & (in8 >= half),
        (lane8 >= row_count) & (in8 >= half),
    ]

    slot_degree = own_waves[:slots] + offset

    def forward_lhs(k, first):
        own = slot_row == slot_ref[k]
        reached = slot_degree + start_ref[k]
        if first:
            degree[pl.ds(k, 1), :] = jnp.sum(
                jnp.where(own, reached, 0).astype(F32), axis=0, keepdims=True
            )
        own = own & (reached < NTRUNC)
        pieces = []
        rows = [jnp.where(own, x_ref[pl.ds(k * levels + l, 1), :], 0.0) for l in range(levels)]
        for parity in range(2):
            for l in range(levels):
                for c in range(2):
                    pieces.append(jnp.where(parts[2 * parity + c], rows[l], 0.0))
        return jnp.concatenate(pieces, axis=0).astype(BF16)

    group = chunk_blocks
    for ic in range(lat_chunks):
        cols = pl.ds(ic * LANES, LANES)

        def forward(g, total, cols=cols, first_pass=ic == 0):
            for u in range(0, group, 2):
                k = g * group + u
                lhs = jnp.concatenate(
                    [forward_lhs(k, first_pass), forward_lhs(k + 1, first_pass)], axis=1
                )
                first, second = leg_ref[k, :, cols], leg_ref[k + 1, :, cols]
                rhs = jnp.concatenate([first, first, second, second], axis=0)
                total = total + jnp.dot(lhs, rhs, preferred_element_type=F32)
            return total

        total = lax.fori_loop(
            0, block_count // group, forward, jnp.zeros((2 * levels * pair, LANES), F32)
        )
        for l in range(levels):
            even = total[l * pair : (l + 1) * pair]
            odd = total[(levels + l) * pair : (levels + l + 1) * pair]
            outgoing[(2 * l) * lat_chunks + ic] = (even + odd).astype(BF16)
            outgoing[(2 * l + 1) * lat_chunks + ic] = (even - odd).astype(BF16)
    go_copies = band_copies(outgoing, incoming, go_sems, True)
    incoming[band] = outgoing[band]

    for copy in wave_copies:
        copy.wait()
    row_block = min(wave_rows, 128)
    peers_in = row_block // pair

    def twiddle_rows(t):
        wave = jnp.concatenate([wave_all[t * peers_in + p] for p in range(peers_in)], axis=0)
        lanes = iota((row_block, LANES), 1)
        real = (iota((row_block, LANES), 0) & (pair - 1)) < slots
        cos_c, sin_c = turns(wave * lanes * LANES)
        lead, trail = jnp.where(real, cos_c, -sin_c), jnp.where(real, sin_c, cos_c)
        cos_f, sin_f = turns(wave * lanes)
        rows = pl.ds(t * row_block, row_block)
        for a in range(NLON // LANES):
            values = lead[:, a : a + 1] * cos_f - trail[:, a : a + 1] * sin_f
            twiddle[rows, pl.ds(a * LANES, LANES)] = values.astype(BF16)

    for t in range(wave_rows // row_block):
        twiddle_rows(t)
    for copy in go_copies:
        copy.wait()

    field = jnp.concatenate([incoming[p] for p in range(band_size)], axis=0)
    field = field.astype(F32).T.astype(BF16)
    width = 512

    def drag_block(j, total):
        cols = pl.ds(pl.multiple_of(j * width, width), width)
        table = twiddle[:, cols]
        values = jnp.dot(field, table, preferred_element_type=F32)
        force = (values * jnp.abs(values)).astype(BF16)
        return total + lax.dot_general(table, force, NT, preferred_element_type=F32)

    spectrum = lax.fori_loop(
        0, NLON // width, drag_block, jnp.zeros((wave_rows, LANES), F32), unroll=True
    )
    spectrum = (spectrum * (1.0 / (band_size * slots * math.sqrt(NLON)))).astype(BF16)
    for p in range(band_size):
        leaving[p] = spectrum[p * pair : (p + 1) * pair]
    back_copies = band_copies(leaving, returned, back_sems, True)
    returned[band] = leaving[band]

    modal_rows = chunk_blocks * all_levels
    r_of, c_of = iota((modal_rows, all_levels), 0), iota((modal_rows, all_levels), 1)
    spread = (whole_mod(r_of, all_levels) == c_of).astype(F32).astype(BF16)
    l_of, q_of = iota((all_levels, modal_rows), 0), iota((all_levels, modal_rows), 1)
    level_of = levels * whole_div(q_of, chunk_rows) + whole_mod(q_of, levels)
    collect = (l_of == level_of).astype(F32).astype(BF16)
    left = jnp.dot(spread, inverse_ref[...].astype(BF16), preferred_element_type=F32).astype(BF16)
    left = jnp.dot(left, collect, preferred_element_type=F32)
    r_of, c_of = iota((modal_rows, modal_rows), 0), iota((modal_rows, modal_rows), 1)
    same = whole_div(r_of, all_levels) == whole_div(whole_mod(c_of, chunk_rows), levels)
    to_modes = jnp.where(same, left, 0.0).astype(BF16)
    r_of, c_of = iota((chunk_rows, all_levels), 0), iota((chunk_rows, all_levels), 1)
    spread = (c_of == lev * levels + whole_mod(r_of, levels)).astype(F32).astype(BF16)
    collect = (l_of == whole_mod(q_of, all_levels)).astype(F32).astype(BF16)
    right = jnp.dot(spread, modes_ref[...].astype(BF16), preferred_element_type=F32).astype(BF16)
    right = jnp.dot(right, collect, preferred_element_type=F32)
    r_of, c_of = iota((chunk_rows, modal_rows), 0), iota((chunk_rows, modal_rows), 1)
    same = whole_div(r_of, levels) == whole_div(c_of, all_levels)
    from_modes = jnp.where(same, right, 0.0).astype(BF16)

    mode_row = iota((all_levels, LANES), 0)
    depth = jnp.zeros((all_levels, LANES), F32)
    for a in range(all_levels):
        depth = jnp.where(mode_row == a, depth_ref[a], depth)

    kinds = 4 * levels
    kind_lane = iota((kinds, kinds * slots), 1)
    lane_slot = whole_mod(kind_lane, slots)
    kind = whole_div(kind_lane, slots) == iota((kinds, kinds * slots), 0)

    group = 4 if block_count % 4 == 0 else 2

    def gain_block(g, carry):
        for u in range(group):
            k = g * group + u
            n = degree[pl.ds(k, 1), :]
            growth = n * (n + 1.0) * (1.0 / (NTRUNC * NTRUNC))
            rows = pl.ds(pl.multiple_of(k * all_levels, all_levels), all_levels)
            gain[rows, :] = 1.0 / (1.0 + depth * growth)
            rows = pl.ds(pl.multiple_of(k * 4 * levels, 16), 4 * levels)
            picks[rows, :] = jnp.where(kind & (lane_slot == slot_ref[k]), 1.0, 0.0).astype(BF16)
        return carry

    lax.fori_loop(0, block_count // group, gain_block, 0)
    for copy in back_copies:
        copy.wait()

    for ic in range(lat_chunks):
        columns = [None] * kinds
        weight = -weight_ref[:, ic * LANES : (ic + 1) * LANES]
        for l in range(levels):
            north = returned[(2 * l) * lat_chunks + ic].astype(F32)
            south = returned[(2 * l + 1) * lat_chunks + ic].astype(F32)
            drag_n = drag_ref[2 * l : 2 * l + 1, ic * LANES : (ic + 1) * LANES]
            drag_s = drag_ref[2 * l + 1 : 2 * l + 2, ic * LANES : (ic + 1) * LANES]
            north, south = drag_n * north, drag_s * south
            for parity, value in enumerate((weight * (north + south), weight * (north - south))):
                for c in range(2):
                    at = (parity * 2 + c) * levels + l
                    columns[at] = value[c * slots : (c + 1) * slots]

        picked[ic] = jnp.concatenate(columns, axis=0).astype(BF16)

    def lev_copies(j):
        first = j * chunk_rows
        rows = pl.ds(first if isinstance(j, int) else pl.multiple_of(first, chunk_rows), chunk_rows)
        return [
            pltpu.make_async_remote_copy(
                src_ref=gathered.at[lev, rows],
                dst_ref=gathered.at[lev, rows],
                send_sem=lev_sems.at[0, step, j],
                recv_sem=lev_sems.at[1, step, j],
                device_id={"lev": lax.rem(lev + step, lev_size)},
                device_id_type=MESH,
            )
            for step in range(1, lev_size)
        ]

    def direct_chunk(j, carry):
        pick_rows = pl.ds(pl.multiple_of(j * chunk_blocks * kinds, 16), chunk_blocks * kinds)
        chosen_rows = [
            jnp.dot(picks[pick_rows, :], picked[ic], preferred_element_type=F32).astype(BF16)
            for ic in range(lat_chunks)
        ]
        for u in range(0, chunk_blocks, 2):
            k = j * chunk_blocks + u
            product = None
            for ic in range(lat_chunks):
                cols = pl.ds(ic * LANES, LANES)
                lhs = chosen_rows[ic][u * kinds : (u + 2) * kinds]
                first, second = leg_ref[k, :, cols], leg_ref[k + 1, :, cols]
                rhs = jnp.concatenate([first, first, second, second], axis=0)
                term = lax.dot_general(lhs, rhs, NT, preferred_element_type=F32)
                product = term if product is None else product + term
            for v in range(2):
                own = product[v * 4 * levels : (v + 1) * 4 * levels, v * LANES : (v + 1) * LANES]
                chosen = jnp.where(even_lane, own[: 2 * levels], own[2 * levels :])
                tendency = jnp.where(real_lane, chosen[:levels], chosen[levels:])
                live = degree[pl.ds(k + v, 1), :] < NTRUNC
                rows = pl.ds((k + v) * levels, levels)
                mixed[rows, :] = jnp.where(live, x_ref[rows, :] + tendency, 0.0)
        rows = pl.ds(pl.multiple_of(j * chunk_rows, chunk_rows), chunk_rows)
        gathered[lev, rows, :] = mixed[rows, :].astype(BF16)
        for copy in lev_copies(j):
            copy.start()
        return carry

    lax.fori_loop(0, chunks, direct_chunk, 0)

    def solve_chunk(j):
        rows = pl.ds(j * chunk_rows, chunk_rows)
        columns = jnp.concatenate([gathered[q, rows, :] for q in range(lev_size)], axis=0)
        modal = jnp.dot(to_modes, columns, preferred_element_type=F32)
        gains = gain[pl.ds(j * modal_rows, modal_rows), :]
        out_ref[rows, :] = jnp.dot(
            from_modes, (modal * gains).astype(BF16), preferred_element_type=F32
        )

    middle = (chunks + 1) // 2
    for part in (range(middle), range(middle, chunks)):
        for j in part:
            for copy in lev_copies(j):
                copy.wait()
        for j in part:
            solve_chunk(j)


def on_device(band_size, lev_size, *args):
    spectral, legendre, waves, slot, start, weights, drag, inverse, modes, depths = args
    block_count, levels, columns = spectral.shape
    lat_pairs = legendre.shape[2]
    slots, all_levels = waves.shape[0], inverse.shape[0]
    pair = 2 * slots
    rows = block_count * levels
    chunk_blocks = max(
        n
        for n in range(2, 17, 2)
        if block_count % n == 0 and n * levels % 16 == 0
    )
    chunks = block_count // chunk_blocks
    assert levels * 2 * lat_pairs == band_size * LANES and columns == LANES
    vmem = pl.BlockSpec(memory_space=pltpu.VMEM)
    box = (band_size, pair, LANES)
    result = pl.pallas_call(
        functools.partial(kernel, band_size, lev_size, chunk_blocks),
        out_shape=jax.ShapeDtypeStruct((rows, LANES), F32),
        in_specs=[pl.BlockSpec(memory_space=pltpu.HBM)] * 10,
        out_specs=vmem,
        scratch_shapes=[
            pltpu.VMEM(box, jnp.int32),
            pltpu.VMEM(box, BF16),
            pltpu.VMEM(box, BF16),
            pltpu.VMEM(box, BF16),
            pltpu.VMEM(box, BF16),
            pltpu.VMEM((band_size * pair, NLON), BF16),
            pltpu.VMEM((lat_pairs // LANES, slots * 4 * levels, LANES), BF16),
            pltpu.VMEM((rows * 4, slots * 4 * levels), BF16),
            pltpu.VMEM((block_count, LANES), F32),
            pltpu.VMEM((rows, LANES), F32),
            pltpu.VMEM((lev_size, rows, LANES), BF16),
            pltpu.VMEM((block_count * all_levels, LANES), F32),
            pltpu.SMEM(waves.shape, jnp.int32),
            pltpu.SMEM(slot.shape, jnp.int32),
            pltpu.SMEM(start.shape, jnp.int32),
            pltpu.SMEM(depths.shape, F32),
            pltpu.VMEM((rows, LANES), F32),
            pltpu.VMEM(legendre.shape, BF16),
            pltpu.VMEM((1, lat_pairs), F32),
            pltpu.VMEM((levels * 2, lat_pairs), F32),
            pltpu.VMEM(inverse.shape, F32),
            pltpu.VMEM(modes.shape, F32),
            pltpu.SemaphoreType.DMA((10,)),
            pltpu.SemaphoreType.DMA((2, band_size)),
            pltpu.SemaphoreType.DMA((2, band_size)),
            pltpu.SemaphoreType.DMA((2, band_size)),
            pltpu.SemaphoreType.DMA((2, lev_size, chunks)),
        ],
        compiler_params=pltpu.CompilerParams(
            collective_id=0, has_side_effects=True, vmem_limit_bytes=60 * 2**20
        ),
    )(
        waves,
        slot,
        start,
        depths,
        spectral.reshape(rows, LANES),
        legendre,
        weights.reshape(1, lat_pairs),
        drag.reshape(levels * 2, lat_pairs),
        inverse,
        modes,
    )
    return result.reshape(spectral.shape)


def solution(mesh):
    placed = (
        P("band", "lev", None),
        P("band", None, None),
        P("band"),
        P("band"),
        P("band"),
        P(),
        P("lev", None, None),
        P(),
        P(),
        P(),
    )
    return jax.shard_map(
        functools.partial(on_device, mesh.shape["band"], mesh.shape["lev"]),
        mesh=mesh,
        in_specs=placed,
        out_specs=P("band", "lev", None),
        check_vma=False,
    )
```

```python
import functools
import math

import jax
import jax.numpy as jnp
from jax import lax
from jax.experimental import pallas as pl
from jax.experimental.pallas import tpu as pltpu
from jax.sharding import PartitionSpec as P

NTRUNC = 1280
NLON = 4096
LANES = 128
MESH = pl.DeviceIdType.MESH
NT = (((1,), (1,)), ((), ()))
F32 = jnp.float32
BF16 = jnp.bfloat16


def iota(shape, dim):
    return lax.broadcasted_iota(jnp.int32, shape, dim)


def whole_div(values, divisor):
    return jnp.floor((values.astype(F32) + 0.5) * (1.0 / divisor)).astype(jnp.int32)


def whole_mod(values, divisor):
    return values - divisor * whole_div(values, divisor)


def turns(phase):
    phase = ((phase + NLON // 2) & (NLON - 1)) - NLON // 2
    y = phase.astype(F32) * (math.pi / NLON)
    z = y * y
    sine, cosine = jnp.zeros_like(z), jnp.zeros_like(z)
    for n in reversed(range(7)):
        sine = sine * z + (-1) ** n / math.factorial(2 * n + 1)
        cosine = cosine * z + (-1) ** n / math.factorial(2 * n)
    sine = sine * y
    return 1.0 - 2.0 * sine * sine, 2.0 * sine * cosine


def kernel(
    band_size,
    lev_size,
    chunk_blocks,
    waves_hbm,
    slot_hbm,
    start_hbm,
    depth_hbm,
    x_hbm,
    leg_hbm,
    weight_hbm,
    drag_hbm,
    inverse_hbm,
    modes_hbm,
    out_ref,
    wave_all,
    outgoing,
    incoming,
    leaving,
    returned,
    twiddle,
    picked,
    picks,
    degree,
    mixed,
    gathered,
    gain,
    waves_ref,
    slot_ref,
    start_ref,
    depth_ref,
    x_ref,
    leg_ref,
    weight_ref,
    drag_ref,
    inverse_ref,
    modes_ref,
    load_sems,
    wave_sems,
    go_sems,
    back_sems,
    lev_sems,
):
    band = lax.axis_index("band")
    lev = lax.axis_index("lev")
    block_count, row_count, lat_pairs = leg_ref.shape
    half = row_count // 2
    levels = x_ref.shape[0] // block_count
    all_levels = levels * lev_size
    slots = waves_ref.shape[0]
    pair = 2 * slots
    lat_chunks = lat_pairs // LANES
    wave_rows = band_size * pair
    chunks = block_count // chunk_blocks
    chunk_rows = chunk_blocks * levels

    loads = [
        pltpu.make_async_copy(source, target, load_sems.at[n])
        for n, (source, target) in enumerate(
            (
                (waves_hbm, waves_ref),
                (slot_hbm, slot_ref),
                (start_hbm, start_ref),
                (x_hbm, x_ref),
                (leg_hbm, leg_ref),
                (depth_hbm, depth_ref),
                (weight_hbm, weight_ref),
                (drag_hbm, drag_ref),
                (inverse_hbm, inverse_ref),
                (modes_hbm, modes_ref),
            )
        )
    ]
    barrier = pltpu.get_barrier_semaphore()
    for step in range(1, band_size):
        pl.semaphore_signal(
            barrier, inc=1, device_id={"band": lax.rem(band + step, band_size)}, device_id_type=MESH
        )
    for step in range(1, lev_size):
        pl.semaphore_signal(
            barrier, inc=1, device_id={"lev": lax.rem(lev + step, lev_size)}, device_id_type=MESH
        )

    for load in loads:
        load.start()
    loads[0].wait()
    row16 = iota((pair, LANES), 0)
    own_waves = jnp.zeros((pair, LANES), jnp.int32)
    for s in range(slots):
        own_waves = jnp.where((row16 == s) | (row16 == s + slots), waves_ref[s], own_waves)
    wave_all[band] = own_waves
    pl.semaphore_wait(barrier, band_size + lev_size - 2)

    def band_copies(source, target, sems, by_peer):
        copies = []
        for step in range(1, band_size):
            peer = lax.rem(band + step, band_size)
            copies.append(
                pltpu.make_async_remote_copy(
                    src_ref=source.at[peer] if by_peer else source.at[band],
                    dst_ref=target.at[band],
                    send_sem=sems.at[0, step],
                    recv_sem=sems.at[1, step],
                    device_id={"band": peer},
                    device_id_type=MESH,
                )
            )
        for copy in copies:
            copy.start()
        return copies

    wave_copies = band_copies(wave_all, wave_all, wave_sems, False)
    for load in loads[1:]:
        load.wait()

    lane = iota((1, LANES), 1)
    in_row = jnp.where(lane < row_count, lane, lane - row_count)
    even_lane = in_row < half
    real_lane = lane < row_count
    offset = jnp.where(even_lane, 2 * in_row, 2 * (in_row - half) + 1)

    slot_row = iota((slots, LANES), 0)
    lane8 = iota((slots, LANES), 1)
    in8 = jnp.where(lane8 < row_count, lane8, lane8 - row_count)
    parts = [
        (lane8 < row_count) & (in8 < half),
        (lane8 >= row_count) & (in8 < half),
        (lane8 < row_count) & (in8 >= half),
        (lane8 >= row_count) & (in8 >= half),
    ]

    slot_degree = own_waves[:slots] + offset

    def forward_lhs(k, first):
        own = slot_row == slot_ref[k]
        reached = slot_degree + start_ref[k]
        if first:
            degree[pl.ds(k, 1), :] = jnp.sum(
                jnp.where(own, reached, 0).astype(F32), axis=0, keepdims=True
            )
        own = own & (reached < NTRUNC)
        pieces = []
        rows = [jnp.where(own, x_ref[pl.ds(k * levels + l, 1), :], 0.0) for l in range(levels)]
        for parity in range(2):
            for l in range(levels):
                for c in range(2):
                    pieces.append(jnp.where(parts[2 * parity + c], rows[l], 0.0))
        return jnp.concatenate(pieces, axis=0).astype(BF16)

    group = chunk_blocks
    for ic in range(lat_chunks):
        cols = pl.ds(ic * LANES, LANES)

        def forward(g, total, cols=cols, first_pass=ic == 0):
            for u in range(0, group, 2):
                k = g * group + u
                lhs = jnp.concatenate(
                    [forward_lhs(k, first_pass), forward_lhs(k + 1, first_pass)], axis=1
                )
                first, second = leg_ref[k, :, cols], leg_ref[k + 1, :, cols]
                rhs = jnp.concatenate([first, first, second, second], axis=0)
                total = total + jnp.dot(lhs, rhs, preferred_element_type=F32)
            return total

        total = lax.fori_loop(
            0, block_count // group, forward, jnp.zeros((2 * levels * pair, LANES), F32),
            unroll=lat_chunks == 1,
        )
        for l in range(levels):
            even = total[l * pair : (l + 1) * pair]
            odd = total[(levels + l) * pair : (levels + l + 1) * pair]
            outgoing[(2 * l) * lat_chunks + ic] = (even + odd).astype(BF16)
            outgoing[(2 * l + 1) * lat_chunks + ic] = (even - odd).astype(BF16)
    go_copies = band_copies(outgoing, incoming, go_sems, True)
    incoming[band] = outgoing[band]

    for copy in wave_copies:
        copy.wait()
    row_block = min(wave_rows, 128)
    peers_in = row_block // pair

    def twiddle_rows(t):
        wave = jnp.concatenate([wave_all[t * peers_in + p] for p in range(peers_in)], axis=0)
        lanes = iota((row_block, LANES), 1)
        real = (iota((row_block, LANES), 0) & (pair - 1)) < slots
        cos_c, sin_c = turns(wave * lanes * LANES)
        lead, trail = jnp.where(real, cos_c, -sin_c), jnp.where(real, sin_c, cos_c)
        cos_f, sin_f = turns(wave * lanes)
        rows = pl.ds(t * row_block, row_block)
        for a in range(NLON // LANES):
            values = lead[:, a : a + 1] * cos_f - trail[:, a : a + 1] * sin_f
            twiddle[rows, pl.ds(a * LANES, LANES)] = values.astype(BF16)

    for t in range(wave_rows // row_block):
        twiddle_rows(t)
    for copy in go_copies:
        copy.wait()

    field = jnp.concatenate([incoming[p] for p in range(band_size)], axis=0)
    field = field.astype(F32).T.astype(BF16)
    width = 512

    def drag_block(j, total):
        cols = pl.ds(pl.multiple_of(j * width, width), width)
        table = twiddle[:, cols]
        values = jnp.dot(field, table, preferred_element_type=F32)
        force = (values * jnp.abs(values)).astype(BF16)
        return total + lax.dot_general(table, force, NT, preferred_element_type=F32)

    spectrum = lax.fori_loop(
        0, NLON // width, drag_block, jnp.zeros((wave_rows, LANES), F32), unroll=True
    )
    spectrum = (spectrum * (1.0 / (band_size * slots * math.sqrt(NLON)))).astype(BF16)
    for p in range(band_size):
        leaving[p] = spectrum[p * pair : (p + 1) * pair]
    back_copies = band_copies(leaving, returned, back_sems, True)
    returned[band] = leaving[band]

    modal_rows = chunk_blocks * all_levels
    r_of, c_of = iota((modal_rows, all_levels), 0), iota((modal_rows, all_levels), 1)
    spread = (whole_mod(r_of, all_levels) == c_of).astype(F32).astype(BF16)
    l_of, q_of = iota((all_levels, modal_rows), 0), iota((all_levels, modal_rows), 1)
    level_of = levels * whole_div(q_of, chunk_rows) + whole_mod(q_of, levels)
    collect = (l_of == level_of).astype(F32).astype(BF16)
    left = jnp.dot(spread, inverse_ref[...].astype(BF16), preferred_element_type=F32).astype(BF16)
    left = jnp.dot(left, collect, preferred_element_type=F32)
    r_of, c_of = iota((modal_rows, modal_rows), 0), iota((modal_rows, modal_rows), 1)
    same = whole_div(r_of, all_levels) == whole_div(whole_mod(c_of, chunk_rows), levels)
    to_modes = jnp.where(same, left, 0.0).astype(BF16)
    r_of, c_of = iota((chunk_rows, all_levels), 0), iota((chunk_rows, all_levels), 1)
    spread = (c_of == lev * levels + whole_mod(r_of, levels)).astype(F32).astype(BF16)
    collect = (l_of == whole_mod(q_of, all_levels)).astype(F32).astype(BF16)
    right = jnp.dot(spread, modes_ref[...].astype(BF16), preferred_element_type=F32).astype(BF16)
    right = jnp.dot(right, collect, preferred_element_type=F32)
    r_of, c_of = iota((chunk_rows, modal_rows), 0), iota((chunk_rows, modal_rows), 1)
    same = whole_div(r_of, levels) == whole_div(c_of, all_levels)
    from_modes = jnp.where(same, right, 0.0).astype(BF16)

    mode_row = iota((all_levels, LANES), 0)
    depth = jnp.zeros((all_levels, LANES), F32)
    for a in range(all_levels):
        depth = jnp.where(mode_row == a, depth_ref[a], depth)

    kinds = 4 * levels
    kind_lane = iota((kinds, kinds * slots), 1)
    lane_slot = whole_mod(kind_lane, slots)
    kind = whole_div(kind_lane, slots) == iota((kinds, kinds * slots), 0)

    group = 4 if block_count % 4 == 0 else 2

    def gain_block(g, carry):
        for u in range(group):
            k = g * group + u
            n = degree[pl.ds(k, 1), :]
            growth = n * (n + 1.0) * (1.0 / (NTRUNC * NTRUNC))
            rows = pl.ds(pl.multiple_of(k * all_levels, all_levels), all_levels)
            gain[rows, :] = 1.0 / (1.0 + depth * growth)
            rows = pl.ds(pl.multiple_of(k * 4 * levels, 16), 4 * levels)
            picks[rows, :] = jnp.where(kind & (lane_slot == slot_ref[k]), 1.0, 0.0).astype(BF16)
        return carry

    lax.fori_loop(0, block_count // group, gain_block, 0, unroll=3)
    for copy in back_copies:
        copy.wait()

    for ic in range(lat_chunks):
        columns = [None] * kinds
        weight = -weight_ref[:, ic * LANES : (ic + 1) * LANES]
        for l in range(levels):
            north = returned[(2 * l) * lat_chunks + ic].astype(F32)
            south = returned[(2 * l + 1) * lat_chunks + ic].astype(F32)
            drag_n = drag_ref[2 * l : 2 * l + 1, ic * LANES : (ic + 1) * LANES]
            drag_s = drag_ref[2 * l + 1 : 2 * l + 2, ic * LANES : (ic + 1) * LANES]
            north, south = drag_n * north, drag_s * south
            for parity, value in enumerate((weight * (north + south), weight * (north - south))):
                for c in range(2):
                    at = (parity * 2 + c) * levels + l
                    columns[at] = value[c * slots : (c + 1) * slots]

        picked[ic] = jnp.concatenate(columns, axis=0).astype(BF16)

    def lev_copies(j):
        first = j * chunk_rows
        rows = pl.ds(first if isinstance(j, int) else pl.multiple_of(first, chunk_rows), chunk_rows)
        return [
            pltpu.make_async_remote_copy(
                src_ref=gathered.at[lev, rows],
                dst_ref=gathered.at[lev, rows],
                send_sem=lev_sems.at[0, step, j],
                recv_sem=lev_sems.at[1, step, j],
                device_id={"lev": lax.rem(lev + step, lev_size)},
                device_id_type=MESH,
            )
            for step in range(1, lev_size)
        ]

    def direct_chunk(j, carry):
        pick_rows = pl.ds(pl.multiple_of(j * chunk_blocks * kinds, 16), chunk_blocks * kinds)
        chosen_rows = [
            jnp.dot(picks[pick_rows, :], picked[ic], preferred_element_type=F32).astype(BF16)
            for ic in range(lat_chunks)
        ]
        for u in range(0, chunk_blocks, 2):
            k = j * chunk_blocks + u
            product = None
            for ic in range(lat_chunks):
                cols = pl.ds(ic * LANES, LANES)
                lhs = chosen_rows[ic][u * kinds : (u + 2) * kinds]
                first, second = leg_ref[k, :, cols], leg_ref[k + 1, :, cols]
                rhs = jnp.concatenate([first, first, second, second], axis=0)
                term = lax.dot_general(lhs, rhs, NT, preferred_element_type=F32)
                product = term if product is None else product + term
            for v in range(2):
                own = product[v * 4 * levels : (v + 1) * 4 * levels, v * LANES : (v + 1) * LANES]
                chosen = jnp.where(even_lane, own[: 2 * levels], own[2 * levels :])
                tendency = jnp.where(real_lane, chosen[:levels], chosen[levels:])
                live = degree[pl.ds(k + v, 1), :] < NTRUNC
                rows = pl.ds((k + v) * levels, levels)
                mixed[rows, :] = jnp.where(live, x_ref[rows, :] + tendency, 0.0)
        rows = pl.ds(pl.multiple_of(j * chunk_rows, chunk_rows), chunk_rows)
        gathered[lev, rows, :] = mixed[rows, :].astype(BF16)
        for copy in lev_copies(j):
            copy.start()
        return carry

    lax.fori_loop(0, chunks, direct_chunk, 0)

    def solve_chunk(j):
        rows = pl.ds(j * chunk_rows, chunk_rows)
        columns = jnp.concatenate([gathered[q, rows, :] for q in range(lev_size)], axis=0)
        modal = jnp.dot(to_modes, columns, preferred_element_type=F32)
        gains = gain[pl.ds(j * modal_rows, modal_rows), :]
        out_ref[rows, :] = jnp.dot(
            from_modes, (modal * gains).astype(BF16), preferred_element_type=F32
        )

    middle = (chunks + 1) // 2
    for part in (range(0, 3), range(3, 5), range(5, chunks)):
        for j in part:
            for copy in lev_copies(j):
                copy.wait()
        for j in part:
            solve_chunk(j)


def on_device(band_size, lev_size, *args):
    spectral, legendre, waves, slot, start, weights, drag, inverse, modes, depths = args
    block_count, levels, columns = spectral.shape
    lat_pairs = legendre.shape[2]
    slots, all_levels = waves.shape[0], inverse.shape[0]
    pair = 2 * slots
    rows = block_count * levels
    chunk_blocks = max(
        n
        for n in range(2, 17, 2)
        if block_count % n == 0 and n * levels % 16 == 0
    )
    chunks = block_count // chunk_blocks
    assert levels * 2 * lat_pairs == band_size * LANES and columns == LANES
    vmem = pl.BlockSpec(memory_space=pltpu.VMEM)
    box = (band_size, pair, LANES)
    result = pl.pallas_call(
        functools.partial(kernel, band_size, lev_size, chunk_blocks),
        out_shape=jax.ShapeDtypeStruct((rows, LANES), F32),
        in_specs=[pl.BlockSpec(memory_space=pltpu.HBM)] * 10,
        out_specs=vmem,
        scratch_shapes=[
            pltpu.VMEM(box, jnp.int32),
            pltpu.VMEM(box, BF16),
            pltpu.VMEM(box, BF16),
            pltpu.VMEM(box, BF16),
            pltpu.VMEM(box, BF16),
            pltpu.VMEM((band_size * pair, NLON), BF16),
            pltpu.VMEM((lat_pairs // LANES, slots * 4 * levels, LANES), BF16),
            pltpu.VMEM((rows * 4, slots * 4 * levels), BF16),
            pltpu.VMEM((block_count, LANES), F32),
            pltpu.VMEM((rows, LANES), F32),
            pltpu.VMEM((lev_size, rows, LANES), BF16),
            pltpu.VMEM((block_count * all_levels, LANES), F32),
            pltpu.SMEM(waves.shape, jnp.int32),
            pltpu.SMEM(slot.shape, jnp.int32),
            pltpu.SMEM(start.shape, jnp.int32),
            pltpu.SMEM(depths.shape, F32),
            pltpu.VMEM((rows, LANES), F32),
            pltpu.VMEM(legendre.shape, BF16),
            pltpu.VMEM((1, lat_pairs), F32),
            pltpu.VMEM((levels * 2, lat_pairs), F32),
            pltpu.VMEM(inverse.shape, F32),
            pltpu.VMEM(modes.shape, F32),
            pltpu.SemaphoreType.DMA((10,)),
            pltpu.SemaphoreType.DMA((2, band_size)),
            pltpu.SemaphoreType.DMA((2, band_size)),
            pltpu.SemaphoreType.DMA((2, band_size)),
            pltpu.SemaphoreType.DMA((2, lev_size, chunks)),
        ],
        compiler_params=pltpu.CompilerParams(
            collective_id=0, has_side_effects=True, vmem_limit_bytes=60 * 2**20
        ),
    )(
        waves,
        slot,
        start,
        depths,
        spectral.reshape(rows, LANES),
        legendre,
        weights.reshape(1, lat_pairs),
        drag.reshape(levels * 2, lat_pairs),
        inverse,
        modes,
    )
    return result.reshape(spectral.shape)


def solution(mesh):
    placed = (
        P("band", "lev", None),
        P("band", None, None),
        P("band"),
        P("band"),
        P("band"),
        P(),
        P("lev", None, None),
        P(),
        P(),
        P(),
    )
    return jax.shard_map(
        functools.partial(on_device, mesh.shape["band"], mesh.shape["lev"]),
        mesh=mesh,
        in_specs=placed,
        out_specs=P("band", "lev", None),
        check_vma=False,
    )
```
